1024 devices in a mesh: node: 64 (over z, core), local: 16 (over x, y).
Axes of the slice: x: 4, y: 4, z: 32, core: 2. Of those that a mesh axis runs over, the one named last changes fastest.
Arguments:
- out_grad: bfloat16 [8192, 4, 1792], P('node', None, 'local'), may hold values from -4 to 4
- combine: float32 [8192, 8], P('node'), may hold values from 0.1 to 1
- expert_ids: int32 [8192, 8], P('node'), may hold values from 0 to 255, as said below
- slot_ids: int32 [8192, 8], P('node'), may hold values from 0 to 3, as said below
- kept_mask: int32 [8192, 8], P('node'), may hold values from 0 to 1, as said below
- saved_inputs: bfloat16 [64, 4, 114688], P(None, None, 'node'), may hold values from -6 to 6
- gate_weight: bfloat16 [114688, 2048], P('node', 'local'), may hold values from -0.0625 to 0.0625
- up_weight: bfloat16 [114688, 2048], P('node', 'local'), may hold values from -0.0625 to 0.0625
- down_weight_t: bfloat16 [114688, 2048], P('node', 'local'), may hold values from -0.125 to 0.125
Outputs:
- token_grad: bfloat16 [8192, 4, 1792], P('node', None, 'local')
- grad_gate: bfloat16 [114688, 2048], P('node', 'local')
- grad_up: bfloat16 [114688, 2048], P('node', 'local')
- grad_down_t: bfloat16 [114688, 2048], P('node', 'local')
The draws below stay inside these ranges and needn't reach their ends.
Inputs may be any that keep to these rules, and one draw needn't show every extreme that they name: `expert_ids`: each token names 8 distinct experts, all in at most 4 of the 8 groups of consecutive experts. `slot_ids`: for one node's tokens and one slab expert the kept choices take the slots 0, 1, 2, ... in token order, each once; 0 where kept_mask is 0. `kept_mask`: 1 exactly where the expert is below 16 and fewer than 4 earlier tokens of the same node chose it.
All inputs are finite; a program needn't handle non-finite values.
Results may differ from the reference program's by a relative error of at most 0.025.
Values may be sent and summed in bfloat16 or wider, within the bound.
No kernel may reach another device: no remote copies, remote signals or barrier semaphores. Data moves between devices by JAX's collectives and lax.ppermute only.
A program may use at most 32 MiB of HBM per device.

```python
import math
import jax
import jax.numpy as jnp
from jax import lax

D = 7168
FF = 2048
ROUTED = 256
TOPK = 8
GROUPS = 8
GROUP_TOP = 4
QUARTERS = 4
CAP = 4
TOK_NODE = 128
SLAB = 16
TOKENS = 8192
DQ = 1792
N_NODE = 64
N_LOCAL = 16


def routing_tables(key):
    key_scores = jax.random.fold_in(key, 11)
    key_bias = jax.random.fold_in(key, 12)
    raw_scores = jax.random.randint(key_scores, (TOKENS, ROUTED), 0, 65536, dtype=jnp.int32)
    expert_bias = jax.random.randint(key_bias, (ROUTED,), 0, 65536, dtype=jnp.int32)
    expert_index = jnp.arange(ROUTED, dtype=jnp.int32)
    expert_bias = jnp.where(expert_index < SLAB, expert_bias, 0)
    expert_bias = jnp.where(expert_index == 0, 65536, expert_bias)
    scores = (raw_scores + expert_bias[None, :]) * ROUTED + expert_index[None, :]
    group_best = jnp.max(scores.reshape(TOKENS, GROUPS, ROUTED // GROUPS), axis=2)
    group_values, chosen_groups = lax.top_k(group_best, GROUP_TOP)
    allowed = jnp.any(jnp.arange(GROUPS, dtype=jnp.int32)[None, None, :] == chosen_groups[:, :, None], axis=1)
    allowed = jnp.repeat(allowed, ROUTED // GROUPS, axis=1)
    masked = jnp.where(allowed, scores, -1)
    top_values, chosen = lax.top_k(masked, TOPK)
    chosen = chosen.astype(jnp.int32)
    onehot = (chosen[:, :, None] == jnp.arange(SLAB, dtype=jnp.int32)[None, None, :]).astype(jnp.int32)
    hits = jnp.sum(onehot, axis=1).reshape(TOKENS // TOK_NODE, TOK_NODE, SLAB)
    earlier = (jnp.cumsum(hits, axis=1) - hits).reshape(TOKENS, SLAB)
    rank = jnp.sum(onehot * earlier[:, None, :], axis=2)
    kept = ((chosen < SLAB) & (rank < CAP)).astype(jnp.int32)
    slots = jnp.where(kept == 1, rank, 0).astype(jnp.int32)
    return (chosen, slots, kept)


def draw_expert_ids(key, part):
    tables = routing_tables(key)
    return tables[0]


def draw_slot_ids(key, part):
    tables = routing_tables(key)
    return tables[1]


def draw_kept_mask(key, part):
    tables = routing_tables(key)
    return tables[2]


def block_levels(stream_key, dims, split, least, top_value):
    factor_of, own = 1.0, jax.random.fold_in(stream_key, 6)
    for axis_at, blocks in split:
        steps = jnp.exp(jax.random.uniform(jax.random.fold_in(own, axis_at), (blocks,), jnp.float32, least / len(split), top_value / len(split)))
        factor_of = factor_of * jnp.repeat(steps, dims[axis_at] // blocks).reshape([-1 if axis == axis_at else 1 for axis in range(len(dims))])
    return factor_of


def normal_values(own_key, dims, deviation, bound, cuts=(), kind=jnp.bfloat16):
    drawn = deviation * jax.random.normal(own_key, dims, jnp.float32)
    if cuts:
        drawn = drawn * block_levels(own_key, dims, cuts, -0.22, 0.18)
    return jnp.clip(drawn, -bound, bound).astype(kind)


def setup_inputs(seed: int = 0) -> dict:
    streams_of = jax.random.split(jax.random.key(seed), 10)
    out_grad = normal_values(streams_of[0], (TOKENS, QUARTERS, DQ), 0.3, 4.0, ((0, 64), (2, 16)))
    combine = jnp.clip(jnp.exp(math.log(1.0) - 2.3025851 * jax.random.uniform(streams_of[1], (TOKENS, TOPK), jnp.float32) ** block_levels(streams_of[1], (TOKENS, TOPK), ((0, 64),), -0.2, 0.2)), 0.1, 1.0)
    expert_ids = draw_expert_ids(jax.random.fold_in(streams_of[9], 71), 0)
    slot_ids = draw_slot_ids(jax.random.fold_in(streams_of[9], 71), 0)
    kept_mask = draw_kept_mask(jax.random.fold_in(streams_of[9], 71), 0)
    saved_inputs = normal_values(streams_of[5], (N_NODE, CAP, SLAB * D), 1.0, 6.0, ((2, 64),))
    gate_weight = normal_values(streams_of[6], (SLAB * D, FF), D ** -0.5, 0.0625, ((0, 64), (1, 16)))
    up_weight = normal_values(streams_of[7], (SLAB * D, FF), D ** -0.5, 0.0625, ((0, 64), (1, 16)))
    down_weight_t = normal_values(streams_of[8], (SLAB * D, FF), FF ** -0.5, 0.125, ((0, 64), (1, 16)))
    return {"out_grad": out_grad, "combine": combine, "expert_ids": expert_ids, "slot_ids": slot_ids, "kept_mask": kept_mask, "saved_inputs": saved_inputs, "gate_weight": gate_weight, "up_weight": up_weight, "down_weight_t": down_weight_t}


def expert_backward(operands):
    inputs, grads_in, gate_block, up_block, down_block = operands
    pre_gate = jnp.dot(inputs, gate_block, preferred_element_type=jnp.float32)
    pre_up = jnp.dot(inputs, up_block, preferred_element_type=jnp.float32)
    grad_act = jnp.dot(grads_in, down_block, preferred_element_type=jnp.float32)
    gate_sig = jax.nn.sigmoid(pre_gate)
    silu_gate = pre_gate * gate_sig
    activated = (silu_gate * pre_up).astype(jnp.bfloat16)
    grad_pre_gate = (grad_act * pre_up * gate_sig * (1.0 + pre_gate * (1.0 - gate_sig))).astype(jnp.bfloat16)
    grad_pre_up = (grad_act * silu_gate).astype(jnp.bfloat16)
    weight_gate = jnp.dot(inputs.T, grad_pre_gate, preferred_element_type=jnp.float32).astype(jnp.bfloat16)
    weight_up = jnp.dot(inputs.T, grad_pre_up, preferred_element_type=jnp.float32).astype(jnp.bfloat16)
    weight_down = jnp.dot(grads_in.T, activated, preferred_element_type=jnp.float32).astype(jnp.bfloat16)
    row_count = inputs.shape[0]
    slice_width = FF // N_LOCAL
    gate_slices = grad_pre_gate.astype(jnp.float32).reshape(row_count, N_LOCAL, slice_width)
    up_slices = grad_pre_up.astype(jnp.float32).reshape(row_count, N_LOCAL, slice_width)
    gate_cols = gate_block.astype(jnp.float32).reshape(D, N_LOCAL, slice_width)
    up_cols = up_block.astype(jnp.float32).reshape(D, N_LOCAL, slice_width)
    slice_part = jnp.einsum("rjh,djh->jrd", gate_slices, gate_cols) + jnp.einsum("rjh,djh->jrd", up_slices, up_cols)
    slice_part = lax.optimization_barrier(slice_part.astype(jnp.bfloat16))
    expert_grad = jnp.sum(slice_part.astype(jnp.float32), axis=0).astype(jnp.bfloat16)
    return weight_gate, weight_up, weight_down, expert_grad


def reference(out_grad, combine, expert_ids, slot_ids, kept_mask, saved_inputs, gate_weight, up_weight, down_weight_t):
    grads = out_grad.reshape(N_NODE, TOK_NODE, D).astype(jnp.float32)
    route_code = (expert_ids * CAP + slot_ids).reshape(N_NODE, TOK_NODE, TOPK)
    valid = (kept_mask == 1).reshape(N_NODE, TOK_NODE, TOPK)
    weights_node = combine.reshape(N_NODE, TOK_NODE, TOPK)
    targets = jnp.arange(SLAB * CAP, dtype=jnp.int32)

    def dispatch_node(operands):
        grad_rows, code_rows, valid_rows, weight_rows = operands
        matched = (code_rows[:, :, None] == targets[None, None, :]) & valid_rows[:, :, None]
        weighted = jnp.sum(jnp.where(matched, weight_rows[:, :, None], 0.0), axis=1)
        return jnp.dot(weighted.T, grad_rows, precision=lax.Precision.HIGHEST).astype(jnp.bfloat16)

    sent = lax.map(dispatch_node, (grads, route_code, valid, weights_node))
    sent = sent.reshape(N_NODE, SLAB, CAP, D).transpose(1, 0, 2, 3).reshape(SLAB, N_NODE * CAP, D)
    saved = saved_inputs.reshape(N_NODE, CAP, SLAB, D).transpose(2, 0, 1, 3).reshape(SLAB, N_NODE * CAP, D)
    gate_blocks = gate_weight.reshape(SLAB, D, FF)
    up_blocks = up_weight.reshape(SLAB, D, FF)
    down_blocks = down_weight_t.reshape(SLAB, D, FF)
    weight_gate, weight_up, weight_down, expert_grad = lax.map(expert_backward, (saved, sent, gate_blocks, up_blocks, down_blocks))
    expert_grad = expert_grad.reshape(SLAB, N_NODE, CAP, D).transpose(1, 0, 2, 3).reshape(N_NODE, SLAB * CAP, D)

    def combine_node(operands):
        table_rows, code_rows, valid_rows = operands
        matched = (code_rows[:, :, None] == targets[None, None, :]) & valid_rows[:, :, None]
        placed = jnp.sum(jnp.where(matched, 1.0, 0.0), axis=1).astype(jnp.float32)
        return jnp.dot(placed, table_rows.astype(jnp.float32), precision=lax.Precision.HIGHEST).astype(jnp.bfloat16)

    token_grad = lax.map(combine_node, (expert_grad, route_code, valid))
    token_grad = token_grad.reshape(TOKENS, QUARTERS, DQ)
    return (token_grad, weight_gate.reshape(SLAB * D, FF), weight_up.reshape(SLAB * D, FF), weight_down.reshape(SLAB * D, FF))
```

```python
import jax
import jax.numpy as jnp
from jax import lax
from jax.sharding import PartitionSpec as P


def swapped(block, axis, bit):
    count = lax.axis_size(axis)
    route = []
    for low in range(count):
        high = low | 1 << bit
        if high != low and high < count:
            route += [(low, high), (high, low)]
    return lax.ppermute(block, axis, route)


def quarter_sum(part):
    for swap_bit in range(2):
        part = part + swapped(part.astype(jnp.bfloat16), "node", swap_bit).astype(jnp.float32)
    return part


def dot(lhs, rhs, lhs_dim, rhs_dim):
    return lax.dot_general(
        lhs, rhs, (((lhs_dim,), (rhs_dim,)), ((), ())), preferred_element_type=jnp.float32
    )


def per_device(
    out_grad,
    combine,
    expert_ids,
    slot_ids,
    kept_mask,
    saved_inputs,
    gate_weight,
    up_weight,
    down_weight_t,
):
    node_count = lax.axis_size("node")
    local_count = lax.axis_size("local")
    slab_count = node_count // 4
    capacity = saved_inputs.shape[1]
    quarter = saved_inputs.shape[2]
    token_count = out_grad.shape[0]
    piece = out_grad.shape[2]
    hidden = gate_weight.shape[1]
    row_count = node_count * capacity

    targets = jnp.arange(slab_count * capacity, dtype=jnp.int32)
    route_code = expert_ids * capacity + slot_ids
    matched = (route_code[:, :, None] == targets[None, None, :]) & (kept_mask[:, :, None] == 1)
    placed = jnp.sum(jnp.where(matched, 1.0, 0.0), axis=1).astype(jnp.bfloat16)
    slot_weight = jnp.sum(jnp.sum(jnp.where(matched, combine[:, :, None], 0.0), axis=1), axis=0)
    grad_rows = out_grad.reshape(token_count, 4 * piece)
    selected = dot(placed, grad_rows, 0, 0)
    outgoing = selected * slot_weight[:, None]
    outgoing = outgoing.reshape(slab_count, capacity, 4, piece).transpose(0, 2, 1, 3)
    outgoing = outgoing.reshape(node_count, capacity, piece).astype(jnp.bfloat16)
    arrived = lax.all_to_all(outgoing, "node", split_axis=0, concat_axis=0, tiled=True)

    inputs = saved_inputs.reshape(row_count, quarter)
    pre_gate_up = quarter_sum(
        jnp.concatenate([dot(inputs, gate_weight, 1, 0), dot(inputs, up_weight, 1, 0)], axis=1)
    )

    arrived, pre_gate_up = lax.optimization_barrier((arrived, pre_gate_up))
    turned = arrived.reshape(row_count, piece).T
    copies = lax.optimization_barrier(
        jnp.broadcast_to(turned[None], (local_count, piece, row_count))
    )
    grads_in = lax.all_to_all(copies, "local", split_axis=0, concat_axis=0, tiled=True)
    grads_in = grads_in.reshape(quarter, row_count)
    grad_act = quarter_sum(dot(grads_in, down_weight_t, 0, 0))

    pre_gate = pre_gate_up[:, :hidden]
    pre_up = pre_gate_up[:, hidden:]
    gate_sig = jax.nn.sigmoid(pre_gate)
    silu_gate = pre_gate * gate_sig
    activated = (silu_gate * pre_up).astype(jnp.bfloat16)
    gate_slope = pre_up * gate_sig * (1.0 + pre_gate * (1.0 - gate_sig))
    grad_pre_gate = (grad_act * gate_slope).astype(jnp.bfloat16)
    grad_pre_up = (grad_act * silu_gate).astype(jnp.bfloat16)

    partial_value = dot(gate_weight, grad_pre_gate, 1, 1) + dot(up_weight, grad_pre_up, 1, 1)
    partial_value = partial_value.astype(jnp.bfloat16).reshape(local_count, piece, row_count)
    pieces = lax.all_to_all(partial_value, "local", split_axis=0, concat_axis=0, tiled=True)
    summed = jnp.sum(pieces.astype(jnp.float32), axis=0).astype(jnp.bfloat16)
    summed = summed.T.reshape(node_count, capacity, piece)
    returned = lax.all_to_all(summed, "node", split_axis=0, concat_axis=0, tiled=True)

    grad_gate = dot(inputs, grad_pre_gate, 0, 0).astype(jnp.bfloat16)
    grad_up = dot(inputs, grad_pre_up, 0, 0).astype(jnp.bfloat16)
    grad_down_t = dot(grads_in, activated, 1, 0).astype(jnp.bfloat16)

    returned_rows = returned.reshape(slab_count, 4, capacity, piece).transpose(0, 2, 1, 3)
    returned_rows = returned_rows.reshape(slab_count * capacity, 4 * piece)
    token_grad = dot(placed, returned_rows, 1, 0)
    token_grad = token_grad.reshape(token_count, 4, piece).astype(jnp.bfloat16)
    return (token_grad, grad_gate, grad_up, grad_down_t)


def solution(mesh):
    placed = (
        P("node", None, "local"),
        P("node", None),
        P("node", None),
        P("node", None),
        P("node", None),
        P(None, None, "node"),
        P("node", "local"),
        P("node", "local"),
        P("node", "local"),
    )
    return jax.shard_map(
        per_device,
        mesh=mesh,
        in_specs=placed,
        out_specs=(
            P("node", None, "local"),
            P("node", "local"),
            P("node", "local"),
            P("node", "local"),
        ),
        check_vma=False,
    )
```

```python
import jax
import jax.numpy as jnp
from jax import lax
from jax.experimental import pallas as pl
from jax.experimental.pallas import tpu as pltpu
from jax.sharding import PartitionSpec as P


def swapped(block, mask):
    count = lax.axis_size("node")
    return lax.ppermute(block, "node", [(at, at ^ mask) for at in range(count)])


def swapped_parts(block, mask, axis):
    parts = [swapped(part, mask) for part in jnp.split(block, 2, axis=axis)]
    return jnp.concatenate(parts, axis=axis)


def dot(lhs, rhs, lhs_dim, rhs_dim):
    return lax.dot_general(
        lhs, rhs, (((lhs_dim,), (rhs_dim,)), ((), ())), preferred_element_type=jnp.float32
    )


def call(kernel, outs, *args, flops=0):
    read = sum(a.size * a.dtype.itemsize for a in args)
    wrote = sum(o.size * o.dtype.itemsize for o in outs)
    space = pl.BlockSpec(memory_space=pltpu.VMEM)
    return pl.pallas_call(
        kernel,
        out_shape=outs,
        in_specs=[
            pl.BlockSpec(memory_space=pltpu.SMEM) if a.ndim == 1 else space for a in args
        ],
        out_specs=[space] * len(outs),
        compiler_params=pltpu.CompilerParams(vmem_limit_bytes=8 << 20),
        cost_estimate=pl.CostEstimate(
            flops=flops, bytes_accessed=read + wrote, transcendentals=0
        ),
    )(*args)


def rows_of(shape, dim):
    return lax.broadcasted_iota(jnp.int32, shape, dim)


def dispatch_kernel(capacity, ids, slots, kept, combine, grads, out, placed):
    choices, tokens = ids.shape
    rows = placed.shape[0]
    code = jnp.where(kept[...] == 1, ids[...] * capacity + slots[...], -1)
    row = rows_of((rows, tokens), 0)
    target = row // (4 * capacity) * capacity + row % capacity
    ones = jnp.zeros((rows, tokens), jnp.float32)
    weights = jnp.zeros((rows, tokens), jnp.float32)
    for k in range(choices):
        match = code[k : k + 1, :] == target
        ones = ones + jnp.where(match, 1.0, 0.0)
        weights = weights + jnp.where(match, combine[k : k + 1, :], 0.0)
    weight = jnp.sum(weights, axis=1, keepdims=True)
    hot = ones.astype(jnp.bfloat16)
    placed[...] = hot
    total = jnp.zeros(out.shape, jnp.float32)
    of_quarter = rows_of(out.shape, 0) // capacity % 4
    for q in range(4):
        total = jnp.where(of_quarter == q, dot(hot, grads[q], 1, 1), total)
    out[...] = (total * weight).astype(jnp.bfloat16)


def selection(rows, cols, capacity, half):
    row = rows_of((rows, cols), 0)
    col = rows_of((rows, cols), 1)
    keep = (row // (2 * capacity) * capacity + row % capacity == col) & (
        row // capacity % 2 == half
    )
    return jnp.where(keep, 1.0, 0.0).astype(jnp.bfloat16)


def spread_kernel(capacity, arrived, out):
    rows, piece = arrived.shape
    for half in range(2):
        chosen = selection(rows, rows // 2, capacity, half)
        turned = dot(arrived[...], chosen, 0, 0).astype(jnp.bfloat16)
        for at in range(out.shape[0]):
            out[at, pl.ds(half * piece, piece), :] = turned


def hidden_kernel(core, part, other, gate, up, other_gate, other_up, acts, out):
    piece = gate.shape[1]
    hidden = acts.shape[1] // 3
    joined = part[...] + other[...].astype(jnp.float32)
    pre_gate = joined[:, :hidden]
    pre_up = joined[:, hidden : 2 * hidden]
    grad_act = joined[:, 2 * hidden :]
    gate_sig = jax.nn.sigmoid(pre_gate)
    silu_gate = pre_gate * gate_sig
    gate_slope = pre_up * gate_sig * (1.0 + pre_gate * (1.0 - gate_sig))
    grad_gate = (grad_act * gate_slope).astype(jnp.bfloat16)
    grad_up = (grad_act * silu_gate).astype(jnp.bfloat16)
    acts[:, pl.ds(0, hidden)] = grad_gate
    acts[:, pl.ds(hidden, hidden)] = grad_up
    acts[:, pl.ds(2 * hidden, hidden)] = (silu_gate * pre_up).astype(jnp.bfloat16)
    here = pl.multiple_of(core[0] * piece, 16)
    there = pl.multiple_of((1 - core[0]) * piece, 16)
    for start, gates, ups in ((here, gate, up), (there, other_gate, other_up)):
        for at in range(out.shape[0]):
            total = dot(gates[at], grad_gate, 1, 1) + dot(ups[at], grad_up, 1, 1)
            out[at, pl.ds(start, piece), :] = total.astype(jnp.bfloat16)


def sum_kernel(capacity, pieces, out):
    rows, piece = out.shape
    total = pieces[0].astype(jnp.float32)
    for at in range(1, pieces.shape[0]):
        total = total + pieces[at].astype(jnp.float32)
    rounded = total.astype(jnp.bfloat16)
    result = jnp.zeros((rows, piece), jnp.float32)
    for half in range(2):
        chosen = selection(rows, rows // 2, capacity, half)
        result = result + dot(chosen, rounded[half * piece : (half + 1) * piece], 1, 1)
    out[...] = result.astype(jnp.bfloat16)


def combine_kernel(capacity, returned, placed, out):
    hot = placed[...]
    of_quarter = rows_of(hot.shape, 0) // capacity % 4
    for q in range(4):
        mine = jnp.where(of_quarter == q, hot, jnp.zeros_like(hot))
        out[q] = dot(returned[...], mine, 0, 0).astype(jnp.bfloat16)


def by_core(core, own, other):
    return jnp.where(core == 0, own, other), jnp.where(core == 0, other, own)


def per_device(
    out_grad,
    combine,
    expert_ids,
    slot_ids,
    kept_mask,
    saved_inputs,
    gate_weight,
    up_weight,
    down_weight_t,
):
    node_count = lax.axis_size("node")
    local_count = lax.axis_size("local")
    core = lax.axis_index("node") % 2
    chips = [[2 * z + c for z in range(node_count // 2)] for c in range(2)]
    capacity = saved_inputs.shape[1]
    quarter = saved_inputs.shape[2]
    token_count = out_grad.shape[0]
    piece = out_grad.shape[2]
    hidden = gate_weight.shape[1]
    rows = node_count * capacity
    half = rows // 2
    bf16 = lambda *shape: jax.ShapeDtypeStruct(shape, jnp.bfloat16)

    def across_chips(block):
        block = block.reshape(node_count // 2, 2 * capacity, piece)
        block = lax.all_to_all(
            block, "node", split_axis=0, concat_axis=0, tiled=True, axis_index_groups=chips
        )
        return block.reshape(rows, piece)

    outgoing, placed = call(
        lambda *refs: dispatch_kernel(capacity, *refs),
        [bf16(rows, piece), bf16(rows, token_count)],
        expert_ids.T,
        slot_ids.T,
        kept_mask.T,
        combine.T,
        out_grad.transpose(1, 2, 0),
    )
    placed, inputs = lax.optimization_barrier((placed, saved_inputs.reshape(rows, quarter)))
    arrived = across_chips(outgoing)

    pre = jnp.concatenate(
        [dot(inputs, gate_weight, 1, 0), dot(inputs, up_weight, 1, 0)], axis=1
    )
    pre = pre.reshape(node_count // 2, 2, capacity, 2 * hidden).transpose(1, 0, 2, 3)
    pre = pre.reshape(2, half, 2 * hidden)
    pre, away = by_core(core, pre[0], pre[1])
    pre = pre + swapped_parts(away.astype(jnp.bfloat16), 1, 1).astype(jnp.float32)
    arrived, pre = lax.optimization_barrier((arrived, pre))

    (copies,) = call(
        lambda *refs: spread_kernel(capacity, *refs),
        [bf16(local_count, 2 * piece, half)],
        arrived,
    )
    copies, *own_weights = lax.optimization_barrier(
        (copies, gate_weight, up_weight, down_weight_t)
    )
    grads_in = lax.all_to_all(copies, "local", split_axis=0, concat_axis=0, tiled=True)
    other_gate, other_up, other_down = [swapped(own, 1) for own in own_weights]
    grads_in, other_down, pre = lax.optimization_barrier((grads_in, other_down, pre))
    slots_in = grads_in.reshape(local_count, 2, piece, half)
    slots_in, slots_away = by_core(core, slots_in[:, 0], slots_in[:, 1])
    slots_in = slots_in.reshape(quarter, half)
    slots_away = slots_away.reshape(quarter, half)
    part = dot(slots_in, down_weight_t, 0, 0) + dot(slots_away, other_down, 0, 0)
    part = jnp.concatenate([pre, part], axis=1)
    other = swapped(part.astype(jnp.bfloat16), 2)
    acts, partial_value = call(
        hidden_kernel,
        [bf16(half, 3 * hidden), bf16(local_count, 2 * piece, half)],
        core.reshape(1),
        part,
        other,
        *[
            w.reshape(local_count, piece, hidden)
            for w in (gate_weight, up_weight, other_gate, other_up)
        ],
    )

    acts, slots_away, partial_value = lax.optimization_barrier((acts, slots_away, partial_value))
    pieces = lax.all_to_all(partial_value, "local", split_axis=0, concat_axis=0, tiled=True)
    (summed,) = call(
        lambda *refs: sum_kernel(capacity, *refs), [bf16(rows, piece)], pieces
    )
    other_acts = swapped(acts, 1)
    other_slots = swapped(slots_away, 1)
    summed, other_acts, other_slots = lax.optimization_barrier((summed, other_acts, other_slots))
    returned = across_chips(summed)
    all_acts = [
        a.reshape(node_count // 2, capacity, 3 * hidden) for a in by_core(core, acts, other_acts)
    ]
    all_acts = jnp.stack(all_acts, axis=1).reshape(rows, 3 * hidden)
    grad_gate = dot(inputs, all_acts[:, :hidden], 0, 0).astype(jnp.bfloat16)
    grad_up = dot(inputs, all_acts[:, hidden : 2 * hidden], 0, 0).astype(jnp.bfloat16)
    grad_down_t = dot(slots_in, acts[:, 2 * hidden :], 1, 0)
    grad_down_t = grad_down_t + dot(other_slots, other_acts[:, 2 * hidden :], 1, 0)
    grad_down_t = grad_down_t.astype(jnp.bfloat16)

    (token_grad,) = call(
        lambda *refs: combine_kernel(capacity, *refs),
        [bf16(4, piece, token_count)],
        returned,
        placed,
    )
    return (token_grad.transpose(2, 0, 1), grad_gate, grad_up, grad_down_t)


def solution(mesh):
    placed = (
        P("node", None, "local"),
        P("node", None),
        P("node", None),
        P("node", None),
        P("node", None),
        P(None, None, "node"),
        P("node", "local"),
        P("node", "local"),
        P("node", "local"),
    )
    return jax.shard_map(
        per_device,
        mesh=mesh,
        in_specs=placed,
        out_specs=(
            P("node", None, "local"),
            P("node", "local"),
            P("node", "local"),
            P("node", "local"),
        ),
        check_vma=False,
    )
```

```python
import jax
import jax.numpy as jnp
from jax import lax
from jax.experimental import pallas as pl
from jax.experimental.pallas import tpu as pltpu
from jax.sharding import PartitionSpec as P


def swapped(block, mask):
    count = lax.axis_size("node")
    return lax.ppermute(block, "node", [(at, at ^ mask) for at in range(count)])


def swapped_parts(block, mask, axis):
    parts = [swapped(part, mask) for part in jnp.split(block, 2, axis=axis)]
    return jnp.concatenate(parts, axis=axis)


def dot(lhs, rhs, lhs_dim, rhs_dim):
    return lax.dot_general(
        lhs, rhs, (((lhs_dim,), (rhs_dim,)), ((), ())), preferred_element_type=jnp.float32
    )


def call(kernel, outs, *args, flops=0, vmem=8 << 20):
    read = sum(a.size * a.dtype.itemsize for a in args)
    wrote = sum(o.size * o.dtype.itemsize for o in outs)
    space = pl.BlockSpec(memory_space=pltpu.VMEM)
    return pl.pallas_call(
        kernel,
        out_shape=outs,
        in_specs=[
            pl.BlockSpec(memory_space=pltpu.SMEM) if a.ndim == 1 else space for a in args
        ],
        out_specs=[space] * len(outs),
        compiler_params=pltpu.CompilerParams(vmem_limit_bytes=vmem),
        cost_estimate=pl.CostEstimate(
            flops=flops, bytes_accessed=read + wrote, transcendentals=0
        ),
    )(*args)


def rows_of(shape, dim):
    return lax.broadcasted_iota(jnp.int32, shape, dim)


def dispatch_kernel(capacity, ids, slots, kept, combine, grads, out, placed):
    choices, tokens = ids.shape
    rows = placed.shape[0]
    code = jnp.where(kept[...] == 1, ids[...] * capacity + slots[...], -1)
    row = rows_of((rows, tokens), 0)
    target = row // (4 * capacity) * capacity + row % capacity
    ones = jnp.zeros((rows, tokens), jnp.float32)
    weights = jnp.zeros((rows, tokens), jnp.float32)
    for k in range(choices):
        match = code[k : k + 1, :] == target
        ones = ones + jnp.where(match, 1.0, 0.0)
        weights = weights + jnp.where(match, combine[k : k + 1, :], 0.0)
    weight = jnp.sum(weights, axis=1, keepdims=True)
    hot = ones.astype(jnp.bfloat16)
    placed[...] = hot
    total = jnp.zeros(out.shape, jnp.float32)
    of_quarter = rows_of(out.shape, 0) // capacity % 4
    for q in range(4):
        total = jnp.where(of_quarter == q, dot(hot, grads[q], 1, 1), total)
    out[...] = (total * weight).astype(jnp.bfloat16)


def selection(rows, cols, capacity, half):
    row = rows_of((rows, cols), 0)
    col = rows_of((rows, cols), 1)
    keep = (row // (2 * capacity) * capacity + row % capacity == col) & (
        row // capacity % 2 == half
    )
    return jnp.where(keep, 1.0, 0.0).astype(jnp.bfloat16)


def spread_kernel(capacity, arrived, out):
    rows, piece = arrived.shape
    for half in range(2):
        chosen = selection(rows, rows // 2, capacity, half)
        turned = dot(arrived[...], chosen, 0, 0).astype(jnp.bfloat16)
        for at in range(out.shape[0]):
            out[at, pl.ds(half * piece, piece), :] = turned


def starts(core, piece):
    return pl.multiple_of(core[0] * piece, 16), pl.multiple_of((1 - core[0]) * piece, 16)


def pair_kernel(core, own, other, out):
    here, there = starts(core, own.shape[1])
    for at in range(out.shape[0]):
        out[at, pl.ds(here, own.shape[1]), :] = own[at]
        out[at, pl.ds(there, own.shape[1]), :] = other[at]


def hidden_kernel(core, pre, part, other, gate_up, other_gate_up, acts, out):
    piece = gate_up.shape[1]
    hidden = part.shape[1]
    pre_gate = pre[:, :hidden]
    pre_up = pre[:, hidden:]
    grad_act = part[...] + other[...].astype(jnp.float32)
    gate_sig = jax.nn.sigmoid(pre_gate)
    silu_gate = pre_gate * gate_sig
    gate_slope = pre_up * gate_sig * (1.0 + pre_gate * (1.0 - gate_sig))
    grad_gate = (grad_act * gate_slope).astype(jnp.bfloat16)
    grad_up = (grad_act * silu_gate).astype(jnp.bfloat16)
    both = jnp.concatenate([grad_gate, grad_up], axis=1)
    acts[:, pl.ds(0, 2 * hidden)] = both
    acts[:, pl.ds(2 * hidden, hidden)] = (silu_gate * pre_up).astype(jnp.bfloat16)
    here, there = starts(core, piece)
    for start, weights in ((here, gate_up), (there, other_gate_up)):
        for at in range(out.shape[0]):
            out[at, pl.ds(start, piece), :] = dot(weights[at], both, 1, 1).astype(jnp.bfloat16)


def sum_kernel(capacity, pieces, out):
    rows, piece = out.shape
    total = pieces[0].astype(jnp.float32)
    for at in range(1, pieces.shape[0]):
        total = total + pieces[at].astype(jnp.float32)
    rounded = total.astype(jnp.bfloat16)
    result = jnp.zeros((rows, piece), jnp.float32)
    for half in range(2):
        chosen = selection(rows, rows // 2, capacity, half)
        result = result + dot(chosen, rounded[half * piece : (half + 1) * piece], 1, 1)
    out[...] = result.astype(jnp.bfloat16)


def combine_kernel(capacity, returned, placed, out):
    hot = placed[...]
    of_quarter = rows_of(hot.shape, 0) // capacity % 4
    for q in range(4):
        mine = jnp.where(of_quarter == q, hot, jnp.zeros_like(hot))
        out[q] = dot(returned[...], mine, 0, 0).astype(jnp.bfloat16)


def by_core(core, own, other):
    return jnp.where(core == 0, own, other), jnp.where(core == 0, other, own)


def per_device(
    out_grad,
    combine,
    expert_ids,
    slot_ids,
    kept_mask,
    saved_inputs,
    gate_weight,
    up_weight,
    down_weight_t,
):
    node_count = lax.axis_size("node")
    local_count = lax.axis_size("local")
    core = lax.axis_index("node") % 2
    chips = [[2 * z + c for z in range(node_count // 2)] for c in range(2)]
    capacity = saved_inputs.shape[1]
    quarter = saved_inputs.shape[2]
    token_count = out_grad.shape[0]
    piece = out_grad.shape[2]
    hidden = gate_weight.shape[1]
    rows = node_count * capacity
    half = rows // 2
    bf16 = lambda *shape: jax.ShapeDtypeStruct(shape, jnp.bfloat16)

    def across_chips(block):
        block = block.reshape(node_count // 2, 2 * capacity, piece)
        block = lax.all_to_all(
            block, "node", split_axis=0, concat_axis=0, tiled=True, axis_index_groups=chips
        )
        return block.reshape(rows, piece)

    outgoing, placed = call(
        lambda *refs: dispatch_kernel(capacity, *refs),
        [bf16(rows, piece), bf16(rows, token_count)],
        expert_ids.T,
        slot_ids.T,
        kept_mask.T,
        combine.T,
        out_grad.transpose(1, 2, 0),
        vmem=56 << 20,
    )
    placed, inputs, *gate_up = lax.optimization_barrier(
        (placed, saved_inputs.reshape(rows, quarter), gate_weight, up_weight)
    )
    gate_up = jnp.concatenate(gate_up, axis=1)
    arrived = across_chips(outgoing)

    pre = dot(inputs, gate_up, 1, 0)
    pre = pre.reshape(node_count // 2, 2, capacity, 2 * hidden).transpose(1, 0, 2, 3)
    pre = pre.reshape(2, half, 2 * hidden)
    pre, away = by_core(core, pre[0], pre[1])
    pre = pre + swapped_parts(away.astype(jnp.bfloat16), 1, 1).astype(jnp.float32)
    arrived, pre = lax.optimization_barrier((arrived, pre))

    (copies,) = call(
        lambda *refs: spread_kernel(capacity, *refs),
        [bf16(local_count, 2 * piece, half)],
        arrived,
    )
    copies, own_down, gate_up = lax.optimization_barrier((copies, down_weight_t, gate_up))
    grads_in = lax.all_to_all(copies, "local", split_axis=0, concat_axis=0, tiled=True)
    other_down = swapped(own_down, 1)
    other_gate_up = swapped(gate_up, 1)
    other_down, pre = lax.optimization_barrier((other_down, pre))
    pre = pre + swapped(pre.astype(jnp.bfloat16), 2).astype(jnp.float32)
    by_piece = lambda block: block.reshape(local_count, piece, block.shape[1])
    (down_pair,) = call(
        pair_kernel,
        [bf16(local_count, 2 * piece, hidden)],
        core.reshape(1),
        by_piece(own_down),
        by_piece(other_down),
    )
    grads_in, down_pair = lax.optimization_barrier((grads_in, down_pair))
    part = dot(
        grads_in.reshape(2 * quarter, half), down_pair.reshape(2 * quarter, hidden), 0, 0
    )
    other = swapped(part.astype(jnp.bfloat16), 2)
    acts, partial_value = call(
        hidden_kernel,
        [bf16(half, 3 * hidden), bf16(local_count, 2 * piece, half)],
        core.reshape(1),
        pre,
        part,
        other,
        by_piece(gate_up),
        by_piece(other_gate_up),
    )

    slots_in = grads_in.reshape(local_count, 2, piece, half)
    slots_in, slots_away = by_core(core, slots_in[:, 0], slots_in[:, 1])
    slots_in = slots_in.reshape(quarter, half)
    slots_away = slots_away.reshape(quarter, half)
    acts, slots_away, partial_value = lax.optimization_barrier((acts, slots_away, partial_value))
    pieces = lax.all_to_all(partial_value, "local", split_axis=0, concat_axis=0, tiled=True)
    (summed,) = call(
        lambda *refs: sum_kernel(capacity, *refs), [bf16(rows, piece)], pieces
    )
    other_acts = swapped(acts, 1)
    other_slots = swapped(slots_away, 1)
    summed, other_acts, other_slots = lax.optimization_barrier((summed, other_acts, other_slots))
    returned = across_chips(summed)
    all_acts = [
        a.reshape(node_count // 2, capacity, 3 * hidden) for a in by_core(core, acts, other_acts)
    ]
    all_acts = jnp.stack(all_acts, axis=1).reshape(rows, 3 * hidden)
    grad_gate = dot(inputs, all_acts[:, :hidden], 0, 0).astype(jnp.bfloat16)
    grad_up = dot(inputs, all_acts[:, hidden : 2 * hidden], 0, 0).astype(jnp.bfloat16)
    grad_down_t = dot(slots_in, acts[:, 2 * hidden :], 1, 0)
    grad_down_t = grad_down_t + dot(other_slots, other_acts[:, 2 * hidden :], 1, 0)
    grad_down_t = grad_down_t.astype(jnp.bfloat16)

    (token_grad,) = call(
        lambda *refs: combine_kernel(capacity, *refs),
        [bf16(4, piece, token_count)],
        returned,
        placed,
    )
    return (token_grad.transpose(2, 0, 1), grad_gate, grad_up, grad_down_t)


def solution(mesh):
    placed = (
        P("node", None, "local"),
        P("node", None),
        P("node", None),
        P("node", None),
        P("node", None),
        P(None, None, "node"),
        P("node", "local"),
        P("node", "local"),
        P("node", "local"),
    )
    return jax.shard_map(
        per_device,
        mesh=mesh,
        in_specs=placed,
        out_specs=(
            P("node", None, "local"),
            P("node", "local"),
            P("node", "local"),
            P("node", "local"),
        ),
        check_vma=False,
    )
```

```python
import jax
import jax.numpy as jnp
from jax import lax
from jax.experimental import pallas as pl
from jax.experimental.pallas import tpu as pltpu
from jax.sharding import PartitionSpec as P


def swapped(block, mask):
    count = lax.axis_size("node")
    return lax.ppermute(block, "node", [(at, at ^ mask) for at in range(count)])


def swapped_parts(block, mask, axis):
    parts = [swapped(part, mask) for part in jnp.split(block, 2, axis=axis)]
    return jnp.concatenate(parts, axis=axis)


def dot(lhs, rhs, lhs_dim, rhs_dim):
    return lax.dot_general(
        lhs, rhs, (((lhs_dim,), (rhs_dim,)), ((), ())), preferred_element_type=jnp.float32
    )


def call(kernel, outs, *args, flops=0, vmem=8 << 20):
    read = sum(a.size * a.dtype.itemsize for a in args)
    wrote = sum(o.size * o.dtype.itemsize for o in outs)
    space = pl.BlockSpec(memory_space=pltpu.VMEM)
    return pl.pallas_call(
        kernel,
        out_shape=outs,
        in_specs=[
            pl.BlockSpec(memory_space=pltpu.SMEM) if a.ndim == 1 else space for a in args
        ],
        out_specs=[space] * len(outs),
        compiler_params=pltpu.CompilerParams(vmem_limit_bytes=vmem),
        cost_estimate=pl.CostEstimate(
            flops=flops, bytes_accessed=read + wrote, transcendentals=0
        ),
    )(*args)


def rows_of(shape, dim):
    return lax.broadcasted_iota(jnp.int32, shape, dim)


def turned_rows(shape):
    row = rows_of(shape, 0)
    middle = shape[0] // 2
    return jnp.where(row < middle, row + middle, row - middle)


def dispatch_kernel(capacity, ids, slots, kept, combine, grads, out, placed):
    choices, tokens = ids.shape
    rows = placed.shape[0]
    code = jnp.where(kept[...] == 1, ids[...] * capacity + slots[...], -1)
    row = turned_rows((rows, tokens))
    target = row // (4 * capacity) * capacity + row % capacity
    ones = jnp.zeros((rows, tokens), jnp.float32)
    weights = jnp.zeros((rows, tokens), jnp.float32)
    for k in range(choices):
        match = code[k : k + 1, :] == target
        ones = ones + jnp.where(match, 1.0, 0.0)
        weights = weights + jnp.where(match, combine[k : k + 1, :], 0.0)
    weight = jnp.sum(weights, axis=1, keepdims=True)
    hot = ones.astype(jnp.bfloat16)
    placed[...] = hot
    total = jnp.zeros(out.shape, jnp.float32)
    of_quarter = rows_of(out.shape, 0) // capacity % 4
    for q in range(4):
        total = jnp.where(of_quarter == q, dot(hot, grads[q], 1, 1), total)
    out[...] = (total * weight).astype(jnp.bfloat16)


def selection(rows, cols, capacity, half):
    row = turned_rows((rows, cols))
    col = rows_of((rows, cols), 1)
    keep = (row // (2 * capacity) * capacity + row % capacity == col) & (
        row // capacity % 2 == half
    )
    return jnp.where(keep, 1.0, 0.0).astype(jnp.bfloat16)


def spread_kernel(capacity, arrived, out):
    rows, piece = arrived.shape
    for half in range(2):
        chosen = selection(rows, rows // 2, capacity, half)
        turned = dot(arrived[...], chosen, 0, 0).astype(jnp.bfloat16)
        for at in range(out.shape[0]):
            out[at, pl.ds(half * piece, piece), :] = turned


def starts(core, piece):
    return pl.multiple_of(core[0] * piece, 16), pl.multiple_of((1 - core[0]) * piece, 16)


def pair_kernel(core, own, other, out):
    here, there = starts(core, own.shape[1])
    for at in range(out.shape[0]):
        out[at, pl.ds(here, own.shape[1]), :] = own[at]
        out[at, pl.ds(there, own.shape[1]), :] = other[at]


def hidden_kernel(core, pre, part, other, gate_up, other_gate_up, acts, out):
    piece = gate_up.shape[1]
    hidden = part.shape[1]
    pre_gate = pre[:, :hidden]
    pre_up = pre[:, hidden:]
    grad_act = part[...] + other[...].astype(jnp.float32)
    gate_sig = jax.nn.sigmoid(pre_gate)
    silu_gate = pre_gate * gate_sig
    gate_slope = pre_up * gate_sig * (1.0 + pre_gate * (1.0 - gate_sig))
    grad_gate = (grad_act * gate_slope).astype(jnp.bfloat16)
    grad_up = (grad_act * silu_gate).astype(jnp.bfloat16)
    both = jnp.concatenate([grad_gate, grad_up], axis=1)
    acts[:, pl.ds(0, 2 * hidden)] = both
    acts[:, pl.ds(2 * hidden, hidden)] = (silu_gate * pre_up).astype(jnp.bfloat16)
    here, there = starts(core, piece)
    for start, weights in ((here, gate_up), (there, other_gate_up)):
        for at in range(out.shape[0]):
            out[at, pl.ds(start, piece), :] = dot(weights[at], both, 1, 1).astype(jnp.bfloat16)


def sum_kernel(capacity, pieces, out):
    rows, piece = out.shape
    total = pieces[0].astype(jnp.float32)
    for at in range(1, pieces.shape[0]):
        total = total + pieces[at].astype(jnp.float32)
    rounded = total.astype(jnp.bfloat16)
    result = jnp.zeros((rows, piece), jnp.float32)
    for half in range(2):
        chosen = selection(rows, rows // 2, capacity, half)
        result = result + dot(chosen, rounded[half * piece : (half + 1) * piece], 1, 1)
    out[...] = result.astype(jnp.bfloat16)


def combine_kernel(capacity, returned, placed, out):
    hot = placed[...]
    of_quarter = rows_of(hot.shape, 0) // capacity % 4
    for q in range(4):
        mine = jnp.where(of_quarter == q, hot, jnp.zeros_like(hot))
        out[q] = dot(returned[...], mine, 0, 0).astype(jnp.bfloat16)


def by_core(core, own, other):
    return jnp.where(core == 0, own, other), jnp.where(core == 0, other, own)


def per_device(
    out_grad,
    combine,
    expert_ids,
    slot_ids,
    kept_mask,
    saved_inputs,
    gate_weight,
    up_weight,
    down_weight_t,
):
    node_count = lax.axis_size("node")
    local_count = lax.axis_size("local")
    core = lax.axis_index("node") % 2
    ring = node_count // 2
    chips = [[2 * ((z + ring // 2) % ring) + c for z in range(ring)] for c in range(2)]
    capacity = saved_inputs.shape[1]
    quarter = saved_inputs.shape[2]
    token_count = out_grad.shape[0]
    piece = out_grad.shape[2]
    hidden = gate_weight.shape[1]
    rows = node_count * capacity
    half = rows // 2
    bf16 = lambda *shape: jax.ShapeDtypeStruct(shape, jnp.bfloat16)

    def across_chips(block):
        block = block.reshape(node_count // 2, 2 * capacity, piece)
        block = lax.all_to_all(
            block, "node", split_axis=0, concat_axis=0, tiled=True, axis_index_groups=chips
        )
        return block.reshape(rows, piece)

    outgoing, placed = call(
        lambda *refs: dispatch_kernel(capacity, *refs),
        [bf16(rows, piece), bf16(rows, token_count)],
        expert_ids.T,
        slot_ids.T,
        kept_mask.T,
        combine.T,
        out_grad.transpose(1, 2, 0),
        vmem=56 << 20,
    )
    placed, inputs, *gate_up = lax.optimization_barrier(
        (placed, saved_inputs.reshape(rows, quarter), gate_weight, up_weight)
    )
    gate_up = jnp.concatenate(gate_up, axis=1)
    arrived = across_chips(outgoing)

    pre = dot(inputs, gate_up, 1, 0)
    pre = pre.reshape(node_count // 2, 2, capacity, 2 * hidden).transpose(1, 0, 2, 3)
    pre = pre.reshape(2, half, 2 * hidden)
    pre, away = by_core(core, pre[0], pre[1])
    pre = pre + swapped_parts(away.astype(jnp.bfloat16), 1, 1).astype(jnp.float32)
    arrived, pre = lax.optimization_barrier((arrived, pre))

    (copies,) = call(
        lambda *refs: spread_kernel(capacity, *refs),
        [bf16(local_count, 2 * piece, half)],
        arrived,
    )
    copies, own_down, gate_up = lax.optimization_barrier((copies, down_weight_t, gate_up))
    grads_in = lax.all_to_all(copies, "local", split_axis=0, concat_axis=0, tiled=True)
    other_down = swapped(own_down, 1)
    other_gate_up = swapped(gate_up, 1)
    other_down, pre = lax.optimization_barrier((other_down, pre))
    pre = pre + swapped(pre.astype(jnp.bfloat16), 2).astype(jnp.float32)
    by_piece = lambda block: block.reshape(local_count, piece, block.shape[1])
    (down_pair,) = call(
        pair_kernel,
        [bf16(local_count, 2 * piece, hidden)],
        core.reshape(1),
        by_piece(own_down),
        by_piece(other_down),
    )
    grads_in, down_pair = lax.optimization_barrier((grads_in, down_pair))
    part = dot(
        grads_in.reshape(2 * quarter, half), down_pair.reshape(2 * quarter, hidden), 0, 0
    )
    other = swapped(part.astype(jnp.bfloat16), 2)
    acts, partial_value = call(
        hidden_kernel,
        [bf16(half, 3 * hidden), bf16(local_count, 2 * piece, half)],
        core.reshape(1),
        pre,
        part,
        other,
        by_piece(gate_up),
        by_piece(other_gate_up),
    )

    slots_in = grads_in.reshape(local_count, 2, piece, half)
    slots_in, slots_away = by_core(core, slots_in[:, 0], slots_in[:, 1])
    slots_in = slots_in.reshape(quarter, half)
    slots_away = slots_away.reshape(quarter, half)
    acts, slots_away, partial_value = lax.optimization_barrier((acts, slots_away, partial_value))
    pieces = lax.all_to_all(partial_value, "local", split_axis=0, concat_axis=0, tiled=True)
    (summed,) = call(
        lambda *refs: sum_kernel(capacity, *refs), [bf16(rows, piece)], pieces
    )
    other_acts = swapped(acts, 1)
    other_slots = swapped(slots_away, 1)
    summed, other_acts, other_slots = lax.optimization_barrier((summed, other_acts, other_slots))
    returned = across_chips(summed)
    all_acts = [
        a.reshape(node_count // 2, capacity, 3 * hidden) for a in by_core(core, acts, other_acts)
    ]
    all_acts = jnp.stack(all_acts, axis=1).reshape(rows, 3 * hidden)
    grad_gate = dot(inputs, all_acts[:, :hidden], 0, 0).astype(jnp.bfloat16)
    grad_up = dot(inputs, all_acts[:, hidden : 2 * hidden], 0, 0).astype(jnp.bfloat16)
    grad_down_t = dot(slots_in, acts[:, 2 * hidden :], 1, 0)
    grad_down_t = grad_down_t + dot(other_slots, other_acts[:, 2 * hidden :], 1, 0)
    grad_down_t = grad_down_t.astype(jnp.bfloat16)

    (token_grad,) = call(
        lambda *refs: combine_kernel(capacity, *refs),
        [bf16(4, piece, token_count)],
        returned,
        placed,
    )
    return (token_grad.transpose(2, 0, 1), grad_gate, grad_up, grad_down_t)


def solution(mesh):
    placed = (
        P("node", None, "local"),
        P("node", None),
        P("node", None),
        P("node", None),
        P("node", None),
        P(None, None, "node"),
        P("node", "local"),
        P("node", "local"),
        P("node", "local"),
    )
    return jax.shard_map(
        per_device,
        mesh=mesh,
        in_specs=placed,
        out_specs=(
            P("node", None, "local"),
            P("node", "local"),
            P("node", "local"),
            P("node", "local"),
        ),
        check_vma=False,
    )
```

```python
import jax
import jax.numpy as jnp
from jax import lax
from jax.experimental import pallas as pl
from jax.experimental.pallas import tpu as pltpu
from jax.sharding import PartitionSpec as P


def swapped(block, mask):
    count = lax.axis_size("node")
    return lax.ppermute(block, "node", [(at, at ^ mask) for at in range(count)])


def dot(lhs, rhs, lhs_dim, rhs_dim):
    return lax.dot_general(
        lhs, rhs, (((lhs_dim,), (rhs_dim,)), ((), ())), preferred_element_type=jnp.float32
    )


def call(kernel, outs, *args, flops=0, vmem=8 << 20):
    read = sum(a.size * a.dtype.itemsize for a in args)
    wrote = sum(o.size * o.dtype.itemsize for o in outs)
    space = pl.BlockSpec(memory_space=pltpu.VMEM)
    return pl.pallas_call(
        kernel,
        out_shape=outs,
        in_specs=[
            pl.BlockSpec(memory_space=pltpu.SMEM) if a.ndim == 1 else space for a in args
        ],
        out_specs=[space] * len(outs),
        compiler_params=pltpu.CompilerParams(vmem_limit_bytes=vmem),
        cost_estimate=pl.CostEstimate(
            flops=flops, bytes_accessed=read + wrote, transcendentals=0
        ),
    )(*args)


def rows_of(shape, dim):
    return lax.broadcasted_iota(jnp.int32, shape, dim)


def turned_rows(shape):
    row = rows_of(shape, 0)
    middle = shape[0] // 2
    return jnp.where(row < middle, row + middle, row - middle)


def dispatch_kernel(capacity, ids, slots, kept, combine, grads, out, placed):
    choices, tokens = ids.shape
    rows = placed.shape[0]
    code = jnp.where(kept[...] == 1, ids[...] * capacity + slots[...], -1)
    row = turned_rows((rows, tokens))
    target = row // (4 * capacity) * capacity + row % capacity
    ones = jnp.zeros((rows, tokens), jnp.float32)
    weights = jnp.zeros((rows, tokens), jnp.float32)
    for k in range(choices):
        match = code[k : k + 1, :] == target
        ones = ones + jnp.where(match, 1.0, 0.0)
        weights = weights + jnp.where(match, combine[k : k + 1, :], 0.0)
    weight = jnp.sum(weights, axis=1, keepdims=True)
    hot = ones.astype(jnp.bfloat16)
    placed[...] = hot
    total = jnp.zeros(out.shape, jnp.float32)
    of_quarter = rows_of(out.shape, 0) // capacity % 4
    for q in range(4):
        total = jnp.where(of_quarter == q, dot(hot, grads[q], 1, 1), total)
    out[...] = (total * weight).astype(jnp.bfloat16)


def selection(rows, cols, capacity, half):
    row = turned_rows((rows, cols))
    col = rows_of((rows, cols), 1)
    keep = (row // (2 * capacity) * capacity + row % capacity == col) & (
        row // capacity % 2 == half
    )
    return jnp.where(keep, 1.0, 0.0).astype(jnp.bfloat16)


def spread_kernel(capacity, arrived, out):
    rows, piece = arrived.shape
    for half in range(2):
        chosen = selection(rows, rows // 2, capacity, half)
        turned = dot(arrived[...], chosen, 0, 0).astype(jnp.bfloat16)
        for at in range(out.shape[0]):
            out[at, pl.ds(half * piece, piece), :] = turned


def starts(core, piece):
    return pl.multiple_of(core[0] * piece, 16), pl.multiple_of((1 - core[0]) * piece, 16)


def pair_kernel(core, own, other, out):
    here, there = starts(core, own.shape[1])
    for at in range(out.shape[0]):
        out[at, pl.ds(here, own.shape[1]), :] = own[at]
        out[at, pl.ds(there, own.shape[1]), :] = other[at]


def hidden_kernel(core, pre, part, other, gate_up, other_gate_up, acts, out):
    piece = gate_up.shape[1]
    hidden = part.shape[1]
    pre_gate = pre[:, :hidden]
    pre_up = pre[:, hidden:]
    grad_act = part[...] + other[...].astype(jnp.float32)
    gate_sig = jax.nn.sigmoid(pre_gate)
    silu_gate = pre_gate * gate_sig
    gate_slope = pre_up * gate_sig * (1.0 + pre_gate * (1.0 - gate_sig))
    grad_gate = (grad_act * gate_slope).astype(jnp.bfloat16)
    grad_up = (grad_act * silu_gate).astype(jnp.bfloat16)
    both = jnp.concatenate([grad_gate, grad_up], axis=1)
    acts[:, pl.ds(0, 2 * hidden)] = both
    acts[:, pl.ds(2 * hidden, hidden)] = (silu_gate * pre_up).astype(jnp.bfloat16)
    here, there = starts(core, piece)
    for start, weights in ((here, gate_up), (there, other_gate_up)):
        for at in range(out.shape[0]):
            out[at, pl.ds(start, piece), :] = dot(weights[at], both, 1, 1).astype(jnp.bfloat16)


def sum_kernel(capacity, pieces, out):
    rows, piece = out.shape
    total = pieces[0].astype(jnp.float32)
    for at in range(1, pieces.shape[0]):
        total = total + pieces[at].astype(jnp.float32)
    rounded = total.astype(jnp.bfloat16)
    result = jnp.zeros((rows, piece), jnp.float32)
    for half in range(2):
        chosen = selection(rows, rows // 2, capacity, half)
        result = result + dot(chosen, rounded[half * piece : (half + 1) * piece], 1, 1)
    out[...] = result.astype(jnp.bfloat16)


def combine_kernel(capacity, returned, placed, out):
    hot = placed[...]
    of_quarter = rows_of(hot.shape, 0) // capacity % 4
    for q in range(4):
        mine = jnp.where(of_quarter == q, hot, jnp.zeros_like(hot))
        out[q] = dot(returned[...], mine, 0, 0).astype(jnp.bfloat16)


def by_core(core, own, other):
    return jnp.where(core == 0, own, other), jnp.where(core == 0, other, own)


def per_device(
    out_grad,
    combine,
    expert_ids,
    slot_ids,
    kept_mask,
    saved_inputs,
    gate_weight,
    up_weight,
    down_weight_t,
):
    node_count = lax.axis_size("node")
    local_count = lax.axis_size("local")
    core = lax.axis_index("node") % 2
    ring = node_count // 2
    chips = [[2 * ((z + ring // 2) % ring) + c for z in range(ring)] for c in range(2)]
    capacity = saved_inputs.shape[1]
    quarter = saved_inputs.shape[2]
    token_count = out_grad.shape[0]
    piece = out_grad.shape[2]
    hidden = gate_weight.shape[1]
    rows = node_count * capacity
    half = rows // 2
    bf16 = lambda *shape: jax.ShapeDtypeStruct(shape, jnp.bfloat16)

    def across_chips(block):
        block = block.reshape(node_count // 2, 2 * capacity, piece)
        block = lax.all_to_all(
            block, "node", split_axis=0, concat_axis=0, tiled=True, axis_index_groups=chips
        )
        return block.reshape(rows, piece)

    outgoing, placed = call(
        lambda *refs: dispatch_kernel(capacity, *refs),
        [bf16(rows, piece), bf16(rows, token_count)],
        expert_ids.T,
        slot_ids.T,
        kept_mask.T,
        combine.T,
        out_grad.transpose(1, 2, 0),
        vmem=56 << 20,
    )
    placed, inputs, *gate_up = lax.optimization_barrier(
        (placed, saved_inputs.reshape(rows, quarter), gate_weight, up_weight)
    )
    gate_up = jnp.concatenate(gate_up, axis=1)
    arrived = across_chips(outgoing)

    pre = dot(inputs, gate_up, 1, 0)
    pre = pre.reshape(node_count // 2, 2, capacity, 2 * hidden).transpose(1, 0, 2, 3)
    pre = pre.reshape(2, half, 2 * hidden)
    pre, away = by_core(core, pre[0], pre[1])
    away = away.astype(jnp.bfloat16)
    arrived, pre, away = lax.optimization_barrier((arrived, pre, away))

    (copies,) = call(
        lambda *refs: spread_kernel(capacity, *refs),
        [bf16(local_count, 2 * piece, half)],
        arrived,
    )
    copies, own_down, gate_up, away = lax.optimization_barrier(
        (copies, down_weight_t, gate_up, away)
    )
    grads_in = lax.all_to_all(copies, "local", split_axis=0, concat_axis=0, tiled=True)
    other_down = swapped(own_down, 1)
    other_gate_up = swapped(gate_up, 1)
    pre = pre + swapped(away, 1).astype(jnp.float32)
    other_down, pre = lax.optimization_barrier((other_down, pre))
    pre = pre + swapped(pre.astype(jnp.bfloat16), 2).astype(jnp.float32)
    by_piece = lambda block: block.reshape(local_count, piece, block.shape[1])
    (down_pair,) = call(
        pair_kernel,
        [bf16(local_count, 2 * piece, hidden)],
        core.reshape(1),
        by_piece(own_down),
        by_piece(other_down),
    )
    grads_in, down_pair = lax.optimization_barrier((grads_in, down_pair))
    part = dot(
        grads_in.reshape(2 * quarter, half), down_pair.reshape(2 * quarter, hidden), 0, 0
    )
    other = swapped(part.astype(jnp.bfloat16), 2)
    acts, partial_value = call(
        hidden_kernel,
        [bf16(half, 3 * hidden), bf16(local_count, 2 * piece, half)],
        core.reshape(1),
        pre,
        part,
        other,
        by_piece(gate_up),
        by_piece(other_gate_up),
    )

    slots_in = grads_in.reshape(local_count, 2, piece, half)
    slots_in, slots_away = by_core(core, slots_in[:, 0], slots_in[:, 1])
    slots_in = slots_in.reshape(quarter, half)
    slots_away = slots_away.reshape(quarter, half)
    acts, slots_away, partial_value = lax.optimization_barrier((acts, slots_away, partial_value))
    pieces = lax.all_to_all(partial_value, "local", split_axis=0, concat_axis=0, tiled=True)
    (summed,) = call(
        lambda *refs: sum_kernel(capacity, *refs), [bf16(rows, piece)], pieces
    )
    other_acts = swapped(acts, 1)
    other_slots = swapped(slots_away, 1)
    summed, other_acts, other_slots = lax.optimization_barrier((summed, other_acts, other_slots))
    returned = across_chips(summed)
    all_acts = [
        a.reshape(node_count // 2, capacity, 3 * hidden) for a in by_core(core, acts, other_acts)
    ]
    all_acts = jnp.stack(all_acts, axis=1).reshape(rows, 3 * hidden)
    grad_gate = dot(inputs, all_acts[:, :hidden], 0, 0).astype(jnp.bfloat16)
    grad_up = dot(inputs, all_acts[:, hidden : 2 * hidden], 0, 0).astype(jnp.bfloat16)
    grad_down_t = dot(slots_in, acts[:, 2 * hidden :], 1, 0)
    grad_down_t = grad_down_t + dot(other_slots, other_acts[:, 2 * hidden :], 1, 0)
    grad_down_t = grad_down_t.astype(jnp.bfloat16)

    (token_grad,) = call(
        lambda *refs: combine_kernel(capacity, *refs),
        [bf16(4, piece, token_count)],
        returned,
        placed,
    )
    return (token_grad.transpose(2, 0, 1), grad_gate, grad_up, grad_down_t)


def solution(mesh):
    placed = (
        P("node", None, "local"),
        P("node", None),
        P("node", None),
        P("node", None),
        P("node", None),
        P(None, None, "node"),
        P("node", "local"),
        P("node", "local"),
        P("node", "local"),
    )
    return jax.shard_map(
        per_device,
        mesh=mesh,
        in_specs=placed,
        out_specs=(
            P("node", None, "local"),
            P("node", "local"),
            P("node", "local"),
            P("node", "local"),
        ),
        check_vma=False,
    )
```

```python
import jax
import jax.numpy as jnp
from jax import lax
from jax.experimental import pallas as pl
from jax.experimental.pallas import tpu as pltpu
from jax.sharding import PartitionSpec as P


def swapped(block, mask):
    count = lax.axis_size("node")
    return lax.ppermute(block, "node", [(at, at ^ mask) for at in range(count)])


def dot(lhs, rhs, lhs_dim, rhs_dim):
    return lax.dot_general(
        lhs, rhs, (((lhs_dim,), (rhs_dim,)), ((), ())), preferred_element_type=jnp.float32
    )


def call(kernel, outs, *args, flops=0, vmem=8 << 20):
    read = sum(a.size * a.dtype.itemsize for a in args)
    wrote = sum(o.size * o.dtype.itemsize for o in outs)
    space = pl.BlockSpec(memory_space=pltpu.VMEM)
    return pl.pallas_call(
        kernel,
        out_shape=outs,
        in_specs=[
            pl.BlockSpec(memory_space=pltpu.SMEM) if a.ndim == 1 else space for a in args
        ],
        out_specs=[space] * len(outs),
        compiler_params=pltpu.CompilerParams(vmem_limit_bytes=vmem),
        cost_estimate=pl.CostEstimate(
            flops=flops, bytes_accessed=read + wrote, transcendentals=0
        ),
    )(*args)


def rows_of(shape, dim):
    return lax.broadcasted_iota(jnp.int32, shape, dim)


def turned_rows(shape):
    row = rows_of(shape, 0)
    middle = shape[0] // 2
    return jnp.where(row < middle, row + middle, row - middle)


def dispatch_kernel(capacity, ids, slots, kept, combine, grads, out, placed):
    choices, tokens = ids.shape
    rows = placed.shape[0]
    code = jnp.where(kept[...] == 1, ids[...] * capacity + slots[...], -1)
    row = turned_rows((rows, tokens))
    target = row // (4 * capacity) * capacity + row % capacity
    ones = jnp.zeros((rows, tokens), jnp.float32)
    weights = jnp.zeros((rows, tokens), jnp.float32)
    for k in range(choices):
        match = code[k : k + 1, :] == target
        ones = ones + jnp.where(match, 1.0, 0.0)
        weights = weights + jnp.where(match, combine[k : k + 1, :], 0.0)
    weight = jnp.sum(weights, axis=1, keepdims=True)
    hot = ones.astype(jnp.bfloat16)
    placed[...] = hot
    total = jnp.zeros(out.shape, jnp.float32)
    of_quarter = rows_of(out.shape, 0) // capacity % 4
    for q in range(4):
        total = jnp.where(of_quarter == q, dot(hot, grads[q], 1, 1), total)
    out[...] = (total * weight).astype(jnp.bfloat16)


def selection(rows, cols, capacity, half):
    row = turned_rows((rows, cols))
    col = rows_of((rows, cols), 1)
    keep = (row // (2 * capacity) * capacity + row % capacity == col) & (
        row // capacity % 2 == half
    )
    return jnp.where(keep, 1.0, 0.0).astype(jnp.bfloat16)


def spread_kernel(capacity, arrived, out):
    rows, piece = arrived.shape
    for half in range(2):
        chosen = selection(rows, rows // 2, capacity, half)
        turned = dot(arrived[...], chosen, 0, 0).astype(jnp.bfloat16)
        for at in range(out.shape[0]):
            out[at, pl.ds(half * piece, piece), :] = turned


def starts(core, piece):
    return pl.multiple_of(core[0] * piece, 16), pl.multiple_of((1 - core[0]) * piece, 16)


def pair_kernel(core, own, other, out):
    here, there = starts(core, own.shape[1])
    for at in range(out.shape[0]):
        out[at, pl.ds(here, own.shape[1]), :] = own[at]
        out[at, pl.ds(there, own.shape[1]), :] = other[at]


def hidden_kernel(core, pre, other_pre, part, other, gate_up, other_gate_up, acts, out):
    piece = gate_up.shape[1]
    hidden = part.shape[1]
    joined = pre[...] + other_pre[...].astype(jnp.float32)
    pre_gate = joined[:, :hidden]
    pre_up = joined[:, hidden:]
    grad_act = part[...] + other[...].astype(jnp.float32)
    gate_sig = jax.nn.sigmoid(pre_gate)
    silu_gate = pre_gate * gate_sig
    gate_slope = pre_up * gate_sig * (1.0 + pre_gate * (1.0 - gate_sig))
    grad_gate = (grad_act * gate_slope).astype(jnp.bfloat16)
    grad_up = (grad_act * silu_gate).astype(jnp.bfloat16)
    both = jnp.concatenate([grad_gate, grad_up], axis=1)
    acts[:, pl.ds(0, 2 * hidden)] = both
    acts[:, pl.ds(2 * hidden, hidden)] = (silu_gate * pre_up).astype(jnp.bfloat16)
    here, there = starts(core, piece)
    for start, weights in ((here, gate_up), (there, other_gate_up)):
        for at in range(out.shape[0]):
            out[at, pl.ds(start, piece), :] = dot(weights[at], both, 1, 1).astype(jnp.bfloat16)


def sum_kernel(capacity, pieces, out):
    rows, piece = out.shape
    total = pieces[0].astype(jnp.float32)
    for at in range(1, pieces.shape[0]):
        total = total + pieces[at].astype(jnp.float32)
    rounded = total.astype(jnp.bfloat16)
    result = jnp.zeros((rows, piece), jnp.float32)
    for half in range(2):
        chosen = selection(rows, rows // 2, capacity, half)
        result = result + dot(chosen, rounded[half * piece : (half + 1) * piece], 1, 1)
    out[...] = result.astype(jnp.bfloat16)


def combine_kernel(capacity, returned, placed, out):
    hot = placed[...]
    of_quarter = rows_of(hot.shape, 0) // capacity % 4
    for q in range(4):
        mine = jnp.where(of_quarter == q, hot, jnp.zeros_like(hot))
        out[q] = dot(returned[...], mine, 0, 0).astype(jnp.bfloat16)


def by_core(core, own, other):
    return jnp.where(core == 0, own, other), jnp.where(core == 0, other, own)


def per_device(
    out_grad,
    combine,
    expert_ids,
    slot_ids,
    kept_mask,
    saved_inputs,
    gate_weight,
    up_weight,
    down_weight_t,
):
    node_count = lax.axis_size("node")
    local_count = lax.axis_size("local")
    core = lax.axis_index("node") % 2
    ring = node_count // 2
    chips = [[2 * ((z + ring // 2) % ring) + c for z in range(ring)] for c in range(2)]
    capacity = saved_inputs.shape[1]
    quarter = saved_inputs.shape[2]
    token_count = out_grad.shape[0]
    piece = out_grad.shape[2]
    hidden = gate_weight.shape[1]
    rows = node_count * capacity
    half = rows // 2
    bf16 = lambda *shape: jax.ShapeDtypeStruct(shape, jnp.bfloat16)

    def across_chips(block):
        block = block.reshape(node_count // 2, 2 * capacity, piece)
        block = lax.all_to_all(
            block, "node", split_axis=0, concat_axis=0, tiled=True, axis_index_groups=chips
        )
        return block.reshape(rows, piece)

    outgoing, placed = call(
        lambda *refs: dispatch_kernel(capacity, *refs),
        [bf16(rows, piece), bf16(rows, token_count)],
        expert_ids.T,
        slot_ids.T,
        kept_mask.T,
        combine.T,
        out_grad.transpose(1, 2, 0),
        vmem=56 << 20,
    )
    placed, inputs, *gate_up = lax.optimization_barrier(
        (placed, saved_inputs.reshape(rows, quarter), gate_weight, up_weight)
    )
    gate_up = jnp.concatenate(gate_up, axis=1)
    arrived = across_chips(outgoing)

    pre = dot(inputs, gate_up, 1, 0)
    pre = pre.reshape(node_count // 2, 2, capacity, 2 * hidden).transpose(1, 0, 2, 3)
    pre = pre.reshape(2, half, 2 * hidden)
    pre, away = by_core(core, pre[0], pre[1])
    away = away.astype(jnp.bfloat16)
    arrived, pre, away = lax.optimization_barrier((arrived, pre, away))

    (copies,) = call(
        lambda *refs: spread_kernel(capacity, *refs),
        [bf16(local_count, 2 * piece, half)],
        arrived,
    )
    copies, own_down, gate_up, away = lax.optimization_barrier(
        (copies, down_weight_t, gate_up, away)
    )
    grads_in = lax.all_to_all(copies, "local", split_axis=0, concat_axis=0, tiled=True)
    other_down = swapped(own_down, 1)
    other_gate_up = swapped(gate_up, 1)
    pre = pre + swapped(away, 1).astype(jnp.float32)
    other_down, pre = lax.optimization_barrier((other_down, pre))
    other_pre = swapped(pre.astype(jnp.bfloat16), 2)
    by_piece = lambda block: block.reshape(local_count, piece, block.shape[1])
    (down_pair,) = call(
        pair_kernel,
        [bf16(local_count, 2 * piece, hidden)],
        core.reshape(1),
        by_piece(own_down),
        by_piece(other_down),
    )
    grads_in, down_pair = lax.optimization_barrier((grads_in, down_pair))
    part = dot(
        grads_in.reshape(2 * quarter, half), down_pair.reshape(2 * quarter, hidden), 0, 0
    )
    other = swapped(part.astype(jnp.bfloat16), 2)
    acts, partial_value = call(
        hidden_kernel,
        [bf16(half, 3 * hidden), bf16(local_count, 2 * piece, half)],
        core.reshape(1),
        pre,
        other_pre,
        part,
        other,
        by_piece(gate_up),
        by_piece(other_gate_up),
    )

    slots_in = grads_in.reshape(local_count, 2, piece, half)
    slots_in, slots_away = by_core(core, slots_in[:, 0], slots_in[:, 1])
    slots_in = slots_in.reshape(quarter, half)
    slots_away = slots_away.reshape(quarter, half)
    acts, slots_away, partial_value = lax.optimization_barrier((acts, slots_away, partial_value))
    pieces = lax.all_to_all(partial_value, "local", split_axis=0, concat_axis=0, tiled=True)
    (summed,) = call(
        lambda *refs: sum_kernel(capacity, *refs), [bf16(rows, piece)], pieces
    )
    other_acts = swapped(acts, 1)
    other_slots = swapped(slots_away, 1)
    summed, other_acts, other_slots = lax.optimization_barrier((summed, other_acts, other_slots))
    returned = across_chips(summed)
    all_acts = [
        a.reshape(node_count // 2, capacity, 3 * hidden) for a in by_core(core, acts, other_acts)
    ]
    all_acts = jnp.stack(all_acts, axis=1).reshape(rows, 3 * hidden)
    grad_gate = dot(inputs, all_acts[:, :hidden], 0, 0).astype(jnp.bfloat16)
    grad_up = dot(inputs, all_acts[:, hidden : 2 * hidden], 0, 0).astype(jnp.bfloat16)
    grad_down_t = dot(slots_in, acts[:, 2 * hidden :], 1, 0)
    grad_down_t = grad_down_t + dot(other_slots, other_acts[:, 2 * hidden :], 1, 0)
    grad_down_t = grad_down_t.astype(jnp.bfloat16)

    (token_grad,) = call(
        lambda *refs: combine_kernel(capacity, *refs),
        [bf16(4, piece, token_count)],
        returned,
        placed,
    )
    return (token_grad.transpose(2, 0, 1), grad_gate, grad_up, grad_down_t)


def solution(mesh):
    placed = (
        P("node", None, "local"),
        P("node", None),
        P("node", None),
        P("node", None),
        P("node", None),
        P(None, None, "node"),
        P("node", "local"),
        P("node", "local"),
        P("node", "local"),
    )
    return jax.shard_map(
        per_device,
        mesh=mesh,
        in_specs=placed,
        out_specs=(
            P("node", None, "local"),
            P("node", "local"),
            P("node", "local"),
            P("node", "local"),
        ),
        check_vma=False,
    )
```

```python
import jax
import jax.numpy as jnp
from jax import lax
from jax.experimental import pallas as pl
from jax.experimental.pallas import tpu as pltpu
from jax.sharding import PartitionSpec as P


def swapped(block, mask):
    count = lax.axis_size("node")
    return lax.ppermute(block, "node", [(at, at ^ mask) for at in range(count)])


def dot(lhs, rhs, lhs_dim, rhs_dim):
    return lax.dot_general(
        lhs, rhs, (((lhs_dim,), (rhs_dim,)), ((), ())), preferred_element_type=jnp.float32
    )


def call(kernel, outs, *args, flops=0, vmem=8 << 20):
    read = sum(a.size * a.dtype.itemsize for a in args)
    wrote = sum(o.size * o.dtype.itemsize for o in outs)
    space = pl.BlockSpec(memory_space=pltpu.VMEM)
    return pl.pallas_call(
        kernel,
        out_shape=outs,
        in_specs=[
            pl.BlockSpec(memory_space=pltpu.SMEM) if a.ndim == 1 else space for a in args
        ],
        out_specs=[space] * len(outs),
        compiler_params=pltpu.CompilerParams(vmem_limit_bytes=vmem),
        cost_estimate=pl.CostEstimate(
            flops=flops, bytes_accessed=read + wrote, transcendentals=0
        ),
    )(*args)


def rows_of(shape, dim):
    return lax.broadcasted_iota(jnp.int32, shape, dim)


def turned_rows(shape):
    row = rows_of(shape, 0)
    middle = shape[0] // 2
    return jnp.where(row < middle, row + middle, row - middle)


def dispatch_kernel(capacity, ids, slots, kept, combine, grads, out, placed):
    choices, tokens = ids.shape
    rows = placed.shape[0]
    code = jnp.where(kept[...] == 1, ids[...] * capacity + slots[...], -1)
    row = turned_rows((rows, tokens))
    target = row // (4 * capacity) * capacity + row % capacity
    ones = jnp.zeros((rows, tokens), jnp.float32)
    weights = jnp.zeros((rows, tokens), jnp.float32)
    for k in range(choices):
        match = code[k : k + 1, :] == target
        ones = ones + jnp.where(match, 1.0, 0.0)
        weights = weights + jnp.where(match, combine[k : k + 1, :], 0.0)
    weight = jnp.sum(weights, axis=1, keepdims=True)
    hot = ones.astype(jnp.bfloat16)
    placed[...] = hot
    total = jnp.zeros(out.shape, jnp.float32)
    of_quarter = rows_of(out.shape, 0) // capacity % 4
    for q in range(4):
        total = jnp.where(of_quarter == q, dot(hot, grads[q], 1, 1), total)
    out[...] = (total * weight).astype(jnp.bfloat16)


def selection(rows, cols, capacity, half):
    row = turned_rows((rows, cols))
    col = rows_of((rows, cols), 1)
    keep = (row // (2 * capacity) * capacity + row % capacity == col) & (
        row // capacity % 2 == half
    )
    return jnp.where(keep, 1.0, 0.0).astype(jnp.bfloat16)


def spread_kernel(capacity, arrived, out):
    rows, piece = arrived.shape
    for half in range(2):
        chosen = selection(rows, rows // 2, capacity, half)
        turned = dot(arrived[...], chosen, 0, 0).astype(jnp.bfloat16)
        for at in range(out.shape[0]):
            out[at, pl.ds(half * piece, piece), :] = turned


def starts(core, piece):
    return pl.multiple_of(core[0] * piece, 16), pl.multiple_of((1 - core[0]) * piece, 16)


def pair_kernel(core, own, other, out):
    here, there = starts(core, own.shape[1])
    for at in range(out.shape[0]):
        out[at, pl.ds(here, own.shape[1]), :] = own[at]
        out[at, pl.ds(there, own.shape[1]), :] = other[at]


def project_kernel(grads, weights, part, rounded):
    total = jnp.zeros(part.shape, jnp.float32)
    for at in range(grads.shape[0]):
        total = total + dot(grads[at], weights[at], 0, 0)
    part[...] = total
    rounded[...] = total.astype(jnp.bfloat16)


def hidden_kernel(core, pre, other_pre, part, other, gate_up, other_gate_up, acts, out):
    piece = gate_up.shape[1]
    hidden = part.shape[1]
    joined = pre[...] + other_pre[...].astype(jnp.float32)
    pre_gate = joined[:, :hidden]
    pre_up = joined[:, hidden:]
    grad_act = part[...] + other[...].astype(jnp.float32)
    gate_sig = jax.nn.sigmoid(pre_gate)
    silu_gate = pre_gate * gate_sig
    gate_slope = pre_up * gate_sig * (1.0 + pre_gate * (1.0 - gate_sig))
    grad_gate = (grad_act * gate_slope).astype(jnp.bfloat16)
    grad_up = (grad_act * silu_gate).astype(jnp.bfloat16)
    both = jnp.concatenate([grad_gate, grad_up], axis=1)
    acts[:, pl.ds(0, 2 * hidden)] = both
    acts[:, pl.ds(2 * hidden, hidden)] = (silu_gate * pre_up).astype(jnp.bfloat16)
    here, there = starts(core, piece)
    for start, weights in ((here, gate_up), (there, other_gate_up)):
        for at in range(out.shape[0]):
            out[at, pl.ds(start, piece), :] = dot(weights[at], both, 1, 1).astype(jnp.bfloat16)


def sum_kernel(capacity, pieces, out):
    rows, piece = out.shape
    total = pieces[0].astype(jnp.float32)
    for at in range(1, pieces.shape[0]):
        total = total + pieces[at].astype(jnp.float32)
    rounded = total.astype(jnp.bfloat16)
    result = jnp.zeros((rows, piece), jnp.float32)
    for half in range(2):
        chosen = selection(rows, rows // 2, capacity, half)
        result = result + dot(chosen, rounded[half * piece : (half + 1) * piece], 1, 1)
    out[...] = result.astype(jnp.bfloat16)


def combine_kernel(capacity, returned, placed, out):
    hot = placed[...]
    of_quarter = rows_of(hot.shape, 0) // capacity % 4
    for q in range(4):
        mine = jnp.where(of_quarter == q, hot, jnp.zeros_like(hot))
        out[q] = dot(returned[...], mine, 0, 0).astype(jnp.bfloat16)


def by_core(core, own, other):
    return jnp.where(core == 0, own, other), jnp.where(core == 0, other, own)


def per_device(
    out_grad,
    combine,
    expert_ids,
    slot_ids,
    kept_mask,
    saved_inputs,
    gate_weight,
    up_weight,
    down_weight_t,
):
    node_count = lax.axis_size("node")
    local_count = lax.axis_size("local")
    core = lax.axis_index("node") % 2
    ring = node_count // 2
    chips = [[2 * ((z + ring // 2) % ring) + c for z in range(ring)] for c in range(2)]
    capacity = saved_inputs.shape[1]
    quarter = saved_inputs.shape[2]
    token_count = out_grad.shape[0]
    piece = out_grad.shape[2]
    hidden = gate_weight.shape[1]
    rows = node_count * capacity
    half = rows // 2
    bf16 = lambda *shape: jax.ShapeDtypeStruct(shape, jnp.bfloat16)

    def across_chips(block):
        block = block.reshape(node_count // 2, 2 * capacity, piece)
        block = lax.all_to_all(
            block, "node", split_axis=0, concat_axis=0, tiled=True, axis_index_groups=chips
        )
        return block.reshape(rows, piece)

    outgoing, placed = call(
        lambda *refs: dispatch_kernel(capacity, *refs),
        [bf16(rows, piece), bf16(rows, token_count)],
        expert_ids.T,
        slot_ids.T,
        kept_mask.T,
        combine.T,
        out_grad.transpose(1, 2, 0),
        vmem=56 << 20,
    )
    placed, inputs, *gate_up = lax.optimization_barrier(
        (placed, saved_inputs.reshape(rows, quarter), gate_weight, up_weight)
    )
    gate_up = jnp.concatenate(gate_up, axis=1)
    arrived = across_chips(outgoing)

    pre = dot(inputs, gate_up, 1, 0)
    pre = pre.reshape(node_count // 2, 2, capacity, 2 * hidden).transpose(1, 0, 2, 3)
    pre = pre.reshape(2, half, 2 * hidden)
    pre, away = by_core(core, pre[0], pre[1])
    away = away.astype(jnp.bfloat16)
    arrived, pre, away = lax.optimization_barrier((arrived, pre, away))

    (copies,) = call(
        lambda *refs: spread_kernel(capacity, *refs),
        [bf16(local_count, 2 * piece, half)],
        arrived,
    )
    copies, own_down, gate_up, away = lax.optimization_barrier(
        (copies, down_weight_t, gate_up, away)
    )
    grads_in = lax.all_to_all(copies, "local", split_axis=0, concat_axis=0, tiled=True)
    other_down = swapped(own_down, 1)
    other_gate_up = swapped(gate_up, 1)
    pre = pre + swapped(away, 1).astype(jnp.float32)
    other_down, pre = lax.optimization_barrier((other_down, pre))
    other_pre = swapped(pre.astype(jnp.bfloat16), 2)
    by_piece = lambda block: block.reshape(local_count, piece, block.shape[1])
    (down_pair,) = call(
        pair_kernel,
        [bf16(local_count, 2 * piece, hidden)],
        core.reshape(1),
        by_piece(own_down),
        by_piece(other_down),
    )
    part, rounded = call(
        project_kernel,
        [jax.ShapeDtypeStruct((half, hidden), jnp.float32), bf16(half, hidden)],
        grads_in,
        down_pair,
    )
    other = swapped(rounded, 2)
    acts, partial_value = call(
        hidden_kernel,
        [bf16(half, 3 * hidden), bf16(local_count, 2 * piece, half)],
        core.reshape(1),
        pre,
        other_pre,
        part,
        other,
        by_piece(gate_up),
        by_piece(other_gate_up),
    )

    slots_in = grads_in.reshape(local_count, 2, piece, half)
    slots_in, slots_away = by_core(core, slots_in[:, 0], slots_in[:, 1])
    slots_in = slots_in.reshape(quarter, half)
    slots_away = slots_away.reshape(quarter, half)
    acts, slots_away, partial_value = lax.optimization_barrier((acts, slots_away, partial_value))
    pieces = lax.all_to_all(partial_value, "local", split_axis=0, concat_axis=0, tiled=True)
    (summed,) = call(
        lambda *refs: sum_kernel(capacity, *refs), [bf16(rows, piece)], pieces
    )
    other_acts = swapped(acts, 1)
    other_slots = swapped(slots_away, 1)
    summed, other_acts, other_slots = lax.optimization_barrier((summed, other_acts, other_slots))
    returned = across_chips(summed)
    all_acts = [
        a.reshape(node_count // 2, capacity, 3 * hidden) for a in by_core(core, acts, other_acts)
    ]
    all_acts = jnp.stack(all_acts, axis=1).reshape(rows, 3 * hidden)
    grad_gate = dot(inputs, all_acts[:, :hidden], 0, 0).astype(jnp.bfloat16)
    grad_up = dot(inputs, all_acts[:, hidden : 2 * hidden], 0, 0).astype(jnp.bfloat16)
    grad_down_t = dot(slots_in, acts[:, 2 * hidden :], 1, 0)
    grad_down_t = grad_down_t + dot(other_slots, other_acts[:, 2 * hidden :], 1, 0)
    grad_down_t = grad_down_t.astype(jnp.bfloat16)

    (token_grad,) = call(
        lambda *refs: combine_kernel(capacity, *refs),
        [bf16(4, piece, token_count)],
        returned,
        placed,
    )
    return (token_grad.transpose(2, 0, 1), grad_gate, grad_up, grad_down_t)


def solution(mesh):
    placed = (
        P("node", None, "local"),
        P("node", None),
        P("node", None),
        P("node", None),
        P("node", None),
        P(None, None, "node"),
        P("node", "local"),
        P("node", "local"),
        P("node", "local"),
    )
    return jax.shard_map(
        per_device,
        mesh=mesh,
        in_specs=placed,
        out_specs=(
            P("node", None, "local"),
            P("node", "local"),
            P("node", "local"),
            P("node", "local"),
        ),
        check_vma=False,
    )
```

```python
import jax
import jax.numpy as jnp
from jax import lax
from jax.experimental import pallas as pl
from jax.experimental.pallas import tpu as pltpu
from jax.sharding import PartitionSpec as P


def swapped(block, mask):
    count = lax.axis_size("node")
    return lax.ppermute(block, "node", [(at, at ^ mask) for at in range(count)])


def dot(lhs, rhs, lhs_dim, rhs_dim):
    return lax.dot_general(
        lhs, rhs, (((lhs_dim,), (rhs_dim,)), ((), ())), preferred_element_type=jnp.float32
    )


def call(kernel, outs, *args, flops=0, vmem=8 << 20):
    read = sum(a.size * a.dtype.itemsize for a in args)
    wrote = sum(o.size * o.dtype.itemsize for o in outs)
    space = pl.BlockSpec(memory_space=pltpu.VMEM)
    return pl.pallas_call(
        kernel,
        out_shape=outs,
        in_specs=[
            pl.BlockSpec(memory_space=pltpu.SMEM) if a.ndim == 1 else space for a in args
        ],
        out_specs=[space] * len(outs),
        compiler_params=pltpu.CompilerParams(vmem_limit_bytes=vmem),
        cost_estimate=pl.CostEstimate(
            flops=flops, bytes_accessed=read + wrote, transcendentals=0
        ),
    )(*args)


def rows_of(shape, dim):
    return lax.broadcasted_iota(jnp.int32, shape, dim)


def turned_rows(shape):
    row = rows_of(shape, 0)
    middle = shape[0] // 2
    return jnp.where(row < middle, row + middle, row - middle)


def dispatch_kernel(capacity, ids, slots, kept, combine, grads, out, placed):
    choices, tokens = ids.shape
    rows = placed.shape[0]
    code = jnp.where(kept[...] == 1, ids[...] * capacity + slots[...], -1)
    row = turned_rows((rows, tokens))
    target = row // (4 * capacity) * capacity + row % capacity
    ones = jnp.zeros((rows, tokens), jnp.float32)
    weights = jnp.zeros((rows, tokens), jnp.float32)
    for k in range(choices):
        match = code[k : k + 1, :] == target
        ones = ones + jnp.where(match, 1.0, 0.0)
        weights = weights + jnp.where(match, combine[k : k + 1, :], 0.0)
    weight = jnp.sum(weights, axis=1, keepdims=True)
    hot = ones.astype(jnp.bfloat16)
    placed[...] = hot
    total = jnp.zeros(out.shape, jnp.float32)
    of_quarter = rows_of(out.shape, 0) // capacity % 4
    for q in range(4):
        total = jnp.where(of_quarter == q, dot(hot, grads[q], 1, 1), total)
    out[...] = (total * weight).astype(jnp.bfloat16)


def selection(rows, cols, capacity, half):
    row = turned_rows((rows, cols))
    col = rows_of((rows, cols), 1)
    keep = (row // (2 * capacity) * capacity + row % capacity == col) & (
        row // capacity % 2 == half
    )
    return jnp.where(keep, 1.0, 0.0).astype(jnp.bfloat16)


def spread_kernel(capacity, arrived, out):
    rows, piece = arrived.shape
    for half in range(2):
        chosen = selection(rows, rows // 2, capacity, half)
        turned = dot(arrived[...], chosen, 0, 0).astype(jnp.bfloat16)
        for at in range(out.shape[0]):
            out[at, pl.ds(half * piece, piece), :] = turned


def starts(core, piece):
    return pl.multiple_of(core[0] * piece, 16), pl.multiple_of((1 - core[0]) * piece, 16)


def project_kernel(core, grads, own, other, part, rounded):
    piece = own.shape[1]
    total = jnp.zeros(part.shape, jnp.float32)
    for start, weights in zip(starts(core, piece), (own, other)):
        for at in range(grads.shape[0]):
            total = total + dot(grads[at, pl.ds(start, piece), :], weights[at], 0, 0)
    part[...] = total
    rounded[...] = total.astype(jnp.bfloat16)


def hidden_kernel(core, pre, other_pre, part, other, gate_up, other_gate_up, acts, out):
    piece = gate_up.shape[1]
    hidden = part.shape[1]
    joined = pre[...] + other_pre[...].astype(jnp.float32)
    pre_gate = joined[:, :hidden]
    pre_up = joined[:, hidden:]
    grad_act = part[...] + other[...].astype(jnp.float32)
    gate_sig = jax.nn.sigmoid(pre_gate)
    silu_gate = pre_gate * gate_sig
    gate_slope = pre_up * gate_sig * (1.0 + pre_gate * (1.0 - gate_sig))
    grad_gate = (grad_act * gate_slope).astype(jnp.bfloat16)
    grad_up = (grad_act * silu_gate).astype(jnp.bfloat16)
    both = jnp.concatenate([grad_gate, grad_up], axis=1)
    acts[:, pl.ds(0, 2 * hidden)] = both
    acts[:, pl.ds(2 * hidden, hidden)] = (silu_gate * pre_up).astype(jnp.bfloat16)
    here, there = starts(core, piece)
    for start, weights in ((here, gate_up), (there, other_gate_up)):
        for at in range(out.shape[0]):
            out[at, pl.ds(start, piece), :] = dot(weights[at], both, 1, 1).astype(jnp.bfloat16)


def sum_kernel(capacity, pieces, out):
    rows, piece = out.shape
    total = pieces[0].astype(jnp.float32)
    for at in range(1, pieces.shape[0]):
        total = total + pieces[at].astype(jnp.float32)
    rounded = total.astype(jnp.bfloat16)
    result = jnp.zeros((rows, piece), jnp.float32)
    for half in range(2):
        chosen = selection(rows, rows // 2, capacity, half)
        result = result + dot(chosen, rounded[half * piece : (half + 1) * piece], 1, 1)
    out[...] = result.astype(jnp.bfloat16)


def combine_kernel(capacity, returned, placed, out):
    hot = placed[...]
    of_quarter = rows_of(hot.shape, 0) // capacity % 4
    for q in range(4):
        mine = jnp.where(of_quarter == q, hot, jnp.zeros_like(hot))
        out[q] = dot(returned[...], mine, 0, 0).astype(jnp.bfloat16)


def by_core(core, own, other):
    return jnp.where(core == 0, own, other), jnp.where(core == 0, other, own)


def per_device(
    out_grad,
    combine,
    expert_ids,
    slot_ids,
    kept_mask,
    saved_inputs,
    gate_weight,
    up_weight,
    down_weight_t,
):
    node_count = lax.axis_size("node")
    local_count = lax.axis_size("local")
    core = lax.axis_index("node") % 2
    ring = node_count // 2
    chips = [[2 * ((z + ring // 2) % ring) + c for z in range(ring)] for c in range(2)]
    capacity = saved_inputs.shape[1]
    quarter = saved_inputs.shape[2]
    token_count = out_grad.shape[0]
    piece = out_grad.shape[2]
    hidden = gate_weight.shape[1]
    rows = node_count * capacity
    half = rows // 2
    bf16 = lambda *shape: jax.ShapeDtypeStruct(shape, jnp.bfloat16)

    def across_chips(block):
        block = block.reshape(node_count // 2, 2 * capacity, piece)
        block = lax.all_to_all(
            block, "node", split_axis=0, concat_axis=0, tiled=True, axis_index_groups=chips
        )
        return block.reshape(rows, piece)

    outgoing, placed = call(
        lambda *refs: dispatch_kernel(capacity, *refs),
        [bf16(rows, piece), bf16(rows, token_count)],
        expert_ids.T,
        slot_ids.T,
        kept_mask.T,
        combine.T,
        out_grad.transpose(1, 2, 0),
        vmem=56 << 20,
    )
    placed, inputs, *gate_up = lax.optimization_barrier(
        (placed, saved_inputs.reshape(rows, quarter), gate_weight, up_weight)
    )
    gate_up = jnp.concatenate(gate_up, axis=1)
    arrived = across_chips(outgoing)

    pre = dot(inputs, gate_up, 1, 0)
    pre = pre.reshape(node_count // 2, 2, capacity, 2 * hidden).transpose(1, 0, 2, 3)
    pre = pre.reshape(2, half, 2 * hidden)
    pre, away = by_core(core, pre[0], pre[1])
    away = away.astype(jnp.bfloat16)
    arrived, pre, away = lax.optimization_barrier((arrived, pre, away))

    (copies,) = call(
        lambda *refs: spread_kernel(capacity, *refs),
        [bf16(local_count, 2 * piece, half)],
        arrived,
    )
    copies, own_down, gate_up, away = lax.optimization_barrier(
        (copies, down_weight_t, gate_up, away)
    )
    grads_in = lax.all_to_all(copies, "local", split_axis=0, concat_axis=0, tiled=True)
    other_down = swapped(own_down, 1)
    other_gate_up = swapped(gate_up, 1)
    pre = pre + swapped(away, 1).astype(jnp.float32)
    other_down, pre = lax.optimization_barrier((other_down, pre))
    other_pre = swapped(pre.astype(jnp.bfloat16), 2)
    by_piece = lambda block: block.reshape(local_count, piece, block.shape[1])
    part, rounded = call(
        project_kernel,
        [jax.ShapeDtypeStruct((half, hidden), jnp.float32), bf16(half, hidden)],
        core.reshape(1),
        grads_in,
        by_piece(down_weight_t),
        by_piece(other_down),
    )
    other = swapped(rounded, 2)
    acts, partial_value = call(
        hidden_kernel,
        [bf16(half, 3 * hidden), bf16(local_count, 2 * piece, half)],
        core.reshape(1),
        pre,
        other_pre,
        part,
        other,
        by_piece(gate_up),
        by_piece(other_gate_up),
    )

    slots_in = grads_in.reshape(local_count, 2, piece, half)
    slots_in, slots_away = by_core(core, slots_in[:, 0], slots_in[:, 1])
    slots_in = slots_in.reshape(quarter, half)
    slots_away = slots_away.reshape(quarter, half)
    acts, slots_away, partial_value = lax.optimization_barrier((acts, slots_away, partial_value))
    pieces = lax.all_to_all(partial_value, "local", split_axis=0, concat_axis=0, tiled=True)
    (summed,) = call(
        lambda *refs: sum_kernel(capacity, *refs), [bf16(rows, piece)], pieces
    )
    other_acts = swapped(acts, 1)
    other_slots = swapped(slots_away, 1)
    summed, other_acts, other_slots = lax.optimization_barrier((summed, other_acts, other_slots))
    returned = across_chips(summed)
    all_acts = [
        a.reshape(node_count // 2, capacity, 3 * hidden) for a in by_core(core, acts, other_acts)
    ]
    all_acts = jnp.stack(all_acts, axis=1).reshape(rows, 3 * hidden)
    grad_gate = dot(inputs, all_acts[:, :hidden], 0, 0).astype(jnp.bfloat16)
    grad_up = dot(inputs, all_acts[:, hidden : 2 * hidden], 0, 0).astype(jnp.bfloat16)
    grad_down_t = dot(slots_in, acts[:, 2 * hidden :], 1, 0)
    grad_down_t = grad_down_t + dot(other_slots, other_acts[:, 2 * hidden :], 1, 0)
    grad_down_t = grad_down_t.astype(jnp.bfloat16)

    (token_grad,) = call(
        lambda *refs: combine_kernel(capacity, *refs),
        [bf16(4, piece, token_count)],
        returned,
        placed,
    )
    return (token_grad.transpose(2, 0, 1), grad_gate, grad_up, grad_down_t)


def solution(mesh):
    placed = (
        P("node", None, "local"),
        P("node", None),
        P("node", None),
        P("node", None),
        P("node", None),
        P(None, None, "node"),
        P("node", "local"),
        P("node", "local"),
        P("node", "local"),
    )
    return jax.shard_map(
        per_device,
        mesh=mesh,
        in_specs=placed,
        out_specs=(
            P("node", None, "local"),
            P("node", "local"),
            P("node", "local"),
            P("node", "local"),
        ),
        check_vma=False,
    )
```
